512 devices in a mesh: dp: 64 (over z, y_lo, x), mp: 8 (over y_hi, core).
Axes of the slice: x: 4, y: 8 (y_hi: 4, y_lo: 2; y = y_hi * 2 + y_lo), z: 8, core: 2. Of those that a mesh axis runs over, the one named last changes fastest.
Arguments:
- activations: bfloat16 [49152, 4096], P('dp', 'mp'), may hold values from -16 to 16
- query_rows: bfloat16 [49152, 4096], P('dp', 'mp'), may hold values from -84 to 84
- key_rows: bfloat16 [49152, 1024], P('dp', 'mp'), may hold values from -5 to 5
- true_cotangent: bfloat16 [49152, 4096], P('dp', 'mp'), may hold values from -6 to 6
- sample_cotangent: bfloat16 [49152, 4096], P('dp', 'mp'), may hold values from -6 to 6
- master: float32 [4096, 1024], P('dp', 'mp'), may hold values from -0.09375 to 0.09375
- moment: float32 [4096, 1024], P('dp', 'mp'), may hold values from -6 to 6
- curvature: float32 [4096, 1024], P('dp', 'mp'), may hold values from 5 to 50
Outputs:
- master_next: float32 [4096, 1024], P('dp', 'mp')
- moment_next: float32 [4096, 1024], P('dp', 'mp')
- curvature_next: float32 [4096, 1024], P('dp', 'mp')
- weights_next: bfloat16 [4096, 1024], P(None, 'mp')
The draws below stay inside these ranges and needn't reach their ends.
All inputs are finite; a program needn't handle non-finite values.
Results may differ from the reference program's by a relative error of at most 0.012.
Values may be sent and summed in bfloat16 or wider, within the bound.
No kernel may reach another device: no remote copies, remote signals or barrier semaphores. Data moves between devices by JAX's collectives and lax.ppermute only.
A program may use at most 64 MiB of HBM per device.

```python
import math
import jax
import jax.numpy as jnp
from jax import lax

D = 4096
HQ = 32
KVH = 8
HD = 128
TOK_DEV = 768
TOKENS = 49152


def attention_pair(key):
    keys_all = jax.random.truncated_normal(jax.random.fold_in(key, 101), -4.0, 4.0, (TOKENS, KVH * HD), jnp.float32)
    queries_all = jax.random.truncated_normal(jax.random.fold_in(key, 102), -4.0, 4.0, (TOKENS, HQ * HD), jnp.float32)
    return (keys_all, queries_all)


def draw_key_rows(key, part):
    keys_all, queries_all = attention_pair(key)
    return keys_all.astype(jnp.bfloat16)


def draw_query_rows(key, part):
    keys_all, queries_all = attention_pair(key)
    return queries_all.astype(jnp.bfloat16)


def raised(entries, key, source, target, parts, factor):
    owner, partner = [(jnp.arange(entries.shape[dim]) // (entries.shape[dim] // parts)).reshape([-1 if axis == dim else 1 for axis in range(entries.ndim)]) for dim in (source, target)]
    chosen = jax.random.permutation(key, parts)[partner]
    strong = (owner == chosen) | (owner == (partner + parts // 2) % parts)
    return jnp.where(strong, factor * entries, entries)


def levels(key, extent, split, smallest, top_value):
    gain = 1.0
    for dim, parts in split:
        steps = jax.random.uniform(jax.random.fold_in(jax.random.fold_in(key, 6), dim), (parts,), jnp.float32, smallest / len(split), top_value / len(split))
        gain = gain * jnp.repeat(jnp.exp(steps), extent[dim] // parts).reshape((-1,) + (1,) * (len(extent) - 1 - dim))
    return gain


def normal_values(rng, extent, spread, reach, split=(), dtype=jnp.bfloat16):
    values = spread * jax.random.normal(rng, extent, jnp.float32)
    if split:
        values = values * levels(rng, extent, split, -0.22, 0.18)
    return jnp.clip(values, -reach, reach).astype(dtype)


def noise_with(own_key, shape, scale, reach, cuts, heavy, held_as=jnp.bfloat16):
    array = scale * jax.random.normal(own_key, shape, jnp.float32)
    if cuts:
        array = array * levels(own_key, shape, cuts, -0.22, 0.18)
    return jnp.clip(raised(array, jax.random.fold_in(own_key, 3), *heavy), -reach, reach).astype(held_as)


def setup_inputs(seed: int = 0) -> dict:
    keys = jax.random.split(jax.random.key(seed), 9)
    activations = noise_with(keys[0], (TOKENS, D), 1.0, 16.0, ((0, 64), (1, 8)), (0, 1, 64, 4.0))
    query_rows = draw_query_rows(jax.random.fold_in(keys[8], 71), 0)
    key_rows = draw_key_rows(jax.random.fold_in(keys[8], 71), 0)
    true_cotangent = normal_values(keys[3], (TOKENS, HQ * HD), 1.0, 6.0, ((0, 64), (1, 8)))
    sample_cotangent = normal_values(keys[4], (TOKENS, HQ * HD), 1.0, 6.0, ((0, 64), (1, 8)))
    master = normal_values(keys[5], (D, KVH * HD), D ** -0.5, 0.09375, ((0, 64), (1, 8)), jnp.float32)
    moment = normal_values(keys[6], (D, KVH * HD), 1.0, 6.0, ((0, 64), (1, 8)), jnp.float32)
    curvature = jnp.clip(jnp.exp(math.log(50.0) - 2.3025851 * jax.random.uniform(keys[7], (D, KVH * HD), jnp.float32) ** levels(keys[7], (D, KVH * HD), ((0, 64), (1, 8)), -0.2, 0.2)), 5.0, 50.0)
    return dict(activations=activations, query_rows=query_rows, key_rows=key_rows, true_cotangent=true_cotangent, sample_cotangent=sample_cotangent, master=master, moment=moment, curvature=curvature)


momentum_decay = 0.965
curvature_decay = 0.99
clip_scale = 0.04
learn_rate = 0.0006
weight_decay = 0.1


def sequence_grads(items):
    query_block, key_block, true_block, sample_block = items
    group_size = HQ // KVH
    query_heads = query_block.astype(jnp.float32).reshape(TOK_DEV, KVH, group_size, HD)
    key_heads = key_block.astype(jnp.float32).reshape(TOK_DEV, KVH, HD)
    scores = jnp.einsum("qkgd,skd->kgqs", query_heads, key_heads) * (HD ** -0.5)
    causal = lax.broadcasted_iota(jnp.int32, (TOK_DEV, TOK_DEV), 0) >= lax.broadcasted_iota(jnp.int32, (TOK_DEV, TOK_DEV), 1)
    masked = jnp.where(causal, scores, -jnp.inf)
    highest = jnp.max(masked, axis=-1, keepdims=True)
    powers = jnp.exp(masked - highest)
    attention = (powers / jnp.sum(powers, axis=-1, keepdims=True)).astype(jnp.bfloat16)
    cotangents = jnp.stack((true_block, sample_block)).astype(jnp.float32).reshape(2, TOK_DEV, KVH, group_size, HD)
    value_grads = jnp.einsum("kgqs,cqkgd->sckd", attention.astype(jnp.float32), cotangents)
    return value_grads.astype(jnp.bfloat16)


def reference(activations, query_rows, key_rows, true_cotangent, sample_cotangent, master, moment, curvature):
    seq_count = TOKENS // TOK_DEV
    value_all = lax.map(sequence_grads, (
        query_rows.reshape(seq_count, TOK_DEV, HQ * HD),
        key_rows.reshape(seq_count, TOK_DEV, KVH * HD),
        true_cotangent.reshape(seq_count, TOK_DEV, HQ * HD),
        sample_cotangent.reshape(seq_count, TOK_DEV, HQ * HD)))
    value_all = value_all.reshape(TOKENS, 2 * KVH * HD)
    contract = (((0,), (0,)), ((), ()))
    summed = lax.dot_general(activations, value_all, contract, preferred_element_type=jnp.float32)
    width_all = KVH * HD
    grad_true = summed[:, :width_all]
    grad_sample = summed[:, width_all:]
    moment_next = momentum_decay * moment + (1.0 - momentum_decay) * grad_true
    curvature_next = curvature_decay * curvature + (1.0 - curvature_decay) * grad_sample * grad_sample
    ratio = jnp.clip(moment_next / (clip_scale * curvature_next), -1.0, 1.0)
    master_next = master * (1.0 - learn_rate * weight_decay) - learn_rate * ratio
    weights_next = master_next.astype(jnp.bfloat16)
    return (master_next, moment_next, curvature_next, weights_next)
```

```python
import jax
import jax.numpy as jnp
from jax import lax
from jax.sharding import Mesh, PartitionSpec as P

HQ = 32
KVH = 8
HD = 128

AXES = ("zh", "zl", "yl", "x", "yh", "c")
SIZES = (4, 2, 2, 4, 4, 2)
NEAR = ("zl", "yl", "x")

momentum_decay = 0.965
curvature_decay = 0.99
clip_scale = 0.04
learn_rate = 0.0006
weight_decay = 0.1


def shift(v, axis, size, step):
    return lax.ppermute(v, axis, [(i, (i + step) % size) for i in range(size)])


def attention_grads(query_rows, key_rows, true_cotangent, sample_cotangent):
    tok_count = query_rows.shape[0]
    kv_local = key_rows.shape[1] // HD
    group_size = HQ // KVH
    query_heads = query_rows.reshape(tok_count, kv_local, group_size, HD)
    key_heads = key_rows.reshape(tok_count, kv_local, HD)
    scores = jnp.einsum(
        "qkgd,skd->kgqs", query_heads, key_heads, preferred_element_type=jnp.float32
    ) * HD ** (-0.5)
    causal = lax.broadcasted_iota(jnp.int32, (tok_count, tok_count), 0) >= lax.broadcasted_iota(
        jnp.int32, (tok_count, tok_count), 1
    )
    masked = jnp.where(causal, scores, -jnp.inf)
    highest = jnp.max(masked, axis=-1, keepdims=True)
    powers = jnp.exp(masked - highest)
    attention = (powers / jnp.sum(powers, axis=-1, keepdims=True)).astype(jnp.bfloat16)
    cotangents = jnp.stack((true_cotangent, sample_cotangent)).reshape(
        2, tok_count, kv_local, group_size, HD
    )
    value_grads = jnp.einsum(
        "kgqs,cqkgd->sckd", attention, cotangents, preferred_element_type=jnp.float32
    )
    return value_grads.astype(jnp.bfloat16).reshape(tok_count, 2 * kv_local * HD)


def shards(
    activations, query_rows, key_rows, true_cotangent, sample_cotangent, master, moment, curvature
):
    zh, yh, core = lax.axis_index("zh"), lax.axis_index("yh"), lax.axis_index("c")
    rows, width = master.shape
    state = jnp.concatenate((master, moment, curvature), axis=0)
    states = lax.all_gather(state, ("zh", "zl"), axis=0).reshape(4, 2, 3, rows, width)
    states = lax.dynamic_index_in_dim(states, lax.axis_index("zl"), 1, keepdims=False)
    sibling = shift(activations, "c", 2, 1)
    features = jnp.concatenate(
        (
            jnp.where(core == 0, activations, sibling),
            jnp.where(core == 0, sibling, activations),
        ),
        axis=1,
    )
    own = attention_grads(query_rows, key_rows, true_cotangent, sample_cotangent)
    half = own.shape[0] // 2
    below = shift(own, "yh", 4, 1)
    above = shift(own, "yh", 4, -1)
    far_first = shift(below[:half], "yh", 4, 1)
    far_last = shift(above[half:], "yh", 4, -1)
    far = jnp.concatenate((far_first, far_last), axis=0)
    ring = jnp.stack((own, above, far, below))
    contract = (((0,), (0,)), ((), ()))
    part = jnp.stack(
        [
            lax.dot_general(features, ring[i], contract, preferred_element_type=jnp.float32).astype(
                jnp.bfloat16
            )
            for i in range(4)
        ]
    )
    part = jnp.roll(part, yh, axis=0)
    part = part.reshape(4, 16, rows, 2 * width).transpose(1, 0, 2, 3)
    part = lax.all_to_all(part, NEAR, 0, 0, tiled=True)
    part = jnp.sum(part.astype(jnp.float32), axis=0).astype(jnp.bfloat16)
    part = jnp.broadcast_to(part[None], (4, 4, rows, 2 * width)).reshape(16, rows, 2 * width)
    part = lax.all_to_all(part, ("zh", "yh"), 0, 0, tiled=True)
    summed = jnp.sum(part.reshape(4, 4, rows, 2 * width).astype(jnp.float32), axis=0)
    grad_true = summed[..., :width]
    grad_sample = summed[..., width:]
    moment_next = momentum_decay * states[:, 1] + (1.0 - momentum_decay) * grad_true
    curvature_next = (
        curvature_decay * states[:, 2] + (1.0 - curvature_decay) * grad_sample * grad_sample
    )
    ratio = jnp.clip(moment_next / (clip_scale * curvature_next), -1.0, 1.0)
    master_next = states[:, 0] * (1.0 - learn_rate * weight_decay) - learn_rate * ratio
    weights = master_next.astype(jnp.bfloat16)
    weights = jnp.broadcast_to(weights[None], (16, 4, rows, width))
    weights = lax.all_to_all(weights, NEAR, 0, 0, tiled=True)
    weights_next = weights.transpose(1, 0, 2, 3).reshape(64 * rows, width)
    mine = lambda v: lax.dynamic_index_in_dim(v, zh, 0, keepdims=False)
    return (mine(master_next), mine(moment_next), mine(curvature_next), weights_next)


def solution(mesh):
    fine = Mesh(mesh.devices.reshape(SIZES), AXES)
    dp, mp = AXES[:4], AXES[4:]
    placed = (P(dp, mp),) * 8
    return jax.shard_map(
        shards,
        mesh=fine,
        in_specs=placed,
        out_specs=(P(dp, mp), P(dp, mp), P(dp, mp), P(None, mp)),
        check_vma=False,
    )
```

```python
import math

import jax
import jax.numpy as jnp
from jax import lax
from jax.experimental import pallas as pl
from jax.experimental.pallas import tpu as pltpu
from jax.sharding import Mesh, PartitionSpec as P

HD = 128
TILE = 256

AXES = ("zh", "zl", "yl", "x", "ya", "yb", "c")
SIZES = (4, 2, 2, 4, 2, 2, 2)
NEAR = ("zl", "yl", "x")

momentum_decay = 0.965
curvature_decay = 0.99
clip_scale = 0.04
learn_rate = 0.0006
weight_decay = 0.1


def swap(v, axes, size, flip):
    return lax.ppermute(v, axes, [(i, i ^ flip) for i in range(size)])


def exchange(v, axes):
    return lax.all_to_all(v, axes, 0, 0, tiled=True)


def copies(v, count):
    return jnp.broadcast_to(v[None], (count,) + v.shape)


def attention_kernel(query_ref, key_ref, true_ref, sample_ref, grads_ref):
    tok_count, heads = query_ref.shape[0], query_ref.shape[1] // HD
    to_power = HD ** (-0.5) * math.log2(math.e)
    tiles = tok_count // TILE
    later = lax.broadcasted_iota(jnp.int32, (TILE, TILE), 0) > lax.broadcasted_iota(
        jnp.int32, (TILE, TILE), 1
    )
    totals = [None] * tiles
    for tile in range(tiles):
        start, end = tile * TILE, (tile + 1) * TILE
        attention, cotangents = [], []
        for head in range(heads):
            lanes = slice(head * HD, (head + 1) * HD)
            scores = lax.dot_general(
                key_ref[:end, :],
                query_ref[start:end, lanes],
                (((1,), (1,)), ((), ())),
                preferred_element_type=jnp.float32,
            )
            diagonal = jnp.where(later, -jnp.inf, scores[start:])
            scores = jnp.concatenate((scores[:start], diagonal), axis=0) if start else diagonal
            highest = jnp.max(scores, axis=0, keepdims=True)
            powers = jnp.exp2((scores - highest) * to_power)
            inverse = 1.0 / jnp.sum(powers, axis=0, keepdims=True)
            attention.append((powers * inverse).astype(jnp.bfloat16))
            cotangents.append(
                jnp.concatenate((true_ref[start:end, lanes], sample_ref[start:end, lanes]), axis=1)
            )
        sums = jnp.dot(
            jnp.concatenate(attention, axis=1),
            jnp.concatenate(cotangents, axis=0),
            preferred_element_type=jnp.float32,
        )
        for i in range(tile + 1):
            rows = sums[i * TILE : (i + 1) * TILE]
            totals[i] = rows if totals[i] is None else totals[i] + rows
    for i in range(tiles):
        grads_ref[i * TILE : (i + 1) * TILE, :] = totals[i].astype(grads_ref.dtype)


def attention_grads(query_rows, key_rows, true_cotangent, sample_cotangent):
    whole = pl.BlockSpec(memory_space=pltpu.VMEM)
    return pl.pallas_call(
        attention_kernel,
        in_specs=[whole] * 4,
        out_specs=whole,
        out_shape=jax.ShapeDtypeStruct((key_rows.shape[0], 2 * HD), jnp.bfloat16),
        compiler_params=pltpu.CompilerParams(vmem_limit_bytes=60 * 1024 * 1024),
        cost_estimate=pl.CostEstimate(flops=0, bytes_accessed=0, transcendentals=0),
    )(query_rows, key_rows, true_cotangent, sample_cotangent)


def shards(
    activations, query_rows, key_rows, true_cotangent, sample_cotangent, master, moment, curvature
):
    zh, core = lax.axis_index("zh"), lax.axis_index("c")
    yl, ya, yb = lax.axis_index("yl"), lax.axis_index("ya"), lax.axis_index("yb")
    rows, width = master.shape
    pair = 2 * width
    across = swap(activations, ("ya", "yb"), 4, 3)
    sibling = swap(activations, "c", 2, 1)
    own = attention_grads(query_rows, key_rows, true_cotangent, sample_cotangent)
    state = jnp.stack((master, moment, curvature))
    own, state = lax.optimization_barrier((own, state))
    other = swap(own, "yb", 2, 1)
    moved = tuple(swap(state, "zh", 4, flip) for flip in (1, 2, 3))
    other, across, moved = lax.optimization_barrier((other, across, moved))
    states = jnp.stack((state,) + moved)
    states = jnp.where(zh & 1 == 0, states, jnp.stack([states[i] for i in (1, 0, 3, 2)]))
    states = jnp.where(zh & 2 == 0, states, jnp.stack([states[i] for i in (2, 3, 0, 1)]))

    def whole(half, sibling):
        return jnp.concatenate(
            (jnp.where(core == 0, half, sibling), jnp.where(core == 0, sibling, half)), axis=1
        )

    blocks = whole(activations, sibling), whole(across, swap(across, "c", 2, 1))
    contract = (((0,), (0,)), ((), ()))
    part = [
        lax.dot_general(block, grads, contract, preferred_element_type=jnp.float32)
        for grads in (own, other)
        for block in blocks
    ]
    part = jnp.stack([p.astype(jnp.bfloat16).reshape(16, rows, pair) for p in part], axis=1)
    part, states = lax.optimization_barrier((part, states))
    part = exchange(part, NEAR)
    part = jnp.sum(part.astype(jnp.float32), axis=0).astype(jnp.bfloat16)
    part_own, part_other = part[:2], part[2:]
    part = jnp.stack(
        (jnp.where(yb == 0, part_own, part_other), jnp.where(yb == 0, part_other, part_own))
    )
    part = jnp.broadcast_to(part[None], (4, 2, 2, rows, pair)).reshape(8, 2, rows, pair)
    part = exchange(part, ("zh", "yb"))
    part = jnp.sum(part.reshape(4, 2, 2, rows, pair).astype(jnp.float32), axis=0)
    summed = jnp.where(
        ya == 0,
        jnp.stack((part[0, 0], part[1, 0], part[1, 1], part[0, 1])),
        jnp.stack((part[1, 1], part[0, 1], part[0, 0], part[1, 0])),
    )
    grad_true = summed[..., :width]
    grad_sample = summed[..., width:]
    moment_next = momentum_decay * states[:, 1] + (1.0 - momentum_decay) * grad_true
    curvature_next = (
        curvature_decay * states[:, 2] + (1.0 - curvature_decay) * grad_sample * grad_sample
    )
    ratio = jnp.clip(moment_next / (clip_scale * curvature_next), -1.0, 1.0)
    master_next = states[:, 0] * (1.0 - learn_rate * weight_decay) - learn_rate * ratio
    weights = master_next.astype(jnp.bfloat16)
    weights = exchange(copies(weights, 16), NEAR)
    weights_next = weights.transpose(1, 0, 2, 3).reshape(64 * rows, width)
    mine = lambda v: lax.dynamic_index_in_dim(v, zh, 0, keepdims=False)
    return (mine(master_next), mine(moment_next), mine(curvature_next), weights_next)


def solution(mesh):
    fine = Mesh(mesh.devices.reshape(SIZES), AXES)
    dp, mp = AXES[:4], AXES[4:]
    placed = (P(dp, mp),) * 8
    return jax.shard_map(
        shards,
        mesh=fine,
        in_specs=placed,
        out_specs=(P(dp, mp), P(dp, mp), P(dp, mp), P(None, mp)),
        check_vma=False,
    )
```

```python
import math

import jax
import jax.numpy as jnp
from jax import lax
from jax.experimental import pallas as pl
from jax.experimental.pallas import tpu as pltpu
from jax.sharding import Mesh, PartitionSpec as P

HD = 128
TILE = 256

AXES = ("zh", "zl", "yl", "x", "ya", "yb", "c")
SIZES = (4, 2, 2, 4, 2, 2, 2)
NEAR = ("zl", "yl", "x")

momentum_decay = 0.965
curvature_decay = 0.99
clip_scale = 0.04
learn_rate = 0.0006
weight_decay = 0.1


def swap(v, axes, size, flip):
    return lax.ppermute(v, axes, [(i, i ^ flip) for i in range(size)])


def exchange(v, axes):
    return lax.all_to_all(v, axes, 0, 0, tiled=True)


def copies(v, count):
    return jnp.broadcast_to(v[None], (count,) + v.shape)


def attention_kernel(query_ref, key_ref, true_ref, sample_ref, grads_ref):
    tok_count, heads = query_ref.shape[0], query_ref.shape[1] // HD
    to_power = HD ** (-0.5) * math.log2(math.e)
    tiles = tok_count // TILE
    later = lax.broadcasted_iota(jnp.int32, (TILE, TILE), 0) > lax.broadcasted_iota(
        jnp.int32, (TILE, TILE), 1
    )
    totals = [None] * tiles
    for tile in range(tiles):
        start, end = tile * TILE, (tile + 1) * TILE
        attention, cotangents = [], []
        for head in range(heads):
            lanes = slice(head * HD, (head + 1) * HD)
            scores = lax.dot_general(
                key_ref[:end, :],
                query_ref[start:end, lanes],
                (((1,), (1,)), ((), ())),
                preferred_element_type=jnp.float32,
            )
            diagonal = jnp.where(later, -jnp.inf, scores[start:])
            scores = jnp.concatenate((scores[:start], diagonal), axis=0) if start else diagonal
            highest = jnp.max(scores, axis=0, keepdims=True)
            powers = jnp.exp2((scores - highest) * to_power)
            inverse = 1.0 / jnp.sum(powers, axis=0, keepdims=True)
            attention.append((powers * inverse).astype(jnp.bfloat16))
            cotangents.append(
                jnp.concatenate((true_ref[start:end, lanes], sample_ref[start:end, lanes]), axis=1)
            )
        sums = jnp.dot(
            jnp.concatenate(attention, axis=1),
            jnp.concatenate(cotangents, axis=0),
            preferred_element_type=jnp.float32,
        )
        for i in range(tile + 1):
            rows = sums[i * TILE : (i + 1) * TILE]
            totals[i] = rows if totals[i] is None else totals[i] + rows
    for i in range(tiles):
        grads_ref[i * TILE : (i + 1) * TILE, :] = totals[i].astype(grads_ref.dtype)


def attention_grads(query_rows, key_rows, true_cotangent, sample_cotangent):
    whole = pl.BlockSpec(memory_space=pltpu.VMEM)
    return pl.pallas_call(
        attention_kernel,
        in_specs=[whole] * 4,
        out_specs=whole,
        out_shape=jax.ShapeDtypeStruct((key_rows.shape[0], 2 * HD), jnp.bfloat16),
        compiler_params=pltpu.CompilerParams(vmem_limit_bytes=60 * 1024 * 1024),
        cost_estimate=pl.CostEstimate(flops=0, bytes_accessed=0, transcendentals=0),
    )(query_rows, key_rows, true_cotangent, sample_cotangent)


def update_kernel(place_ref, part_ref, states_ref, master_ref, moment_ref, curvature_ref, weights_ref):
    zh, ya = place_ref[0], place_ref[1]
    width = master_ref.shape[1]
    for yb in range(2):
        for side in range(2):
            block = (2 * ya + yb) ^ (3 * side)
            summed = part_ref[0, yb, side].astype(jnp.float32)
            for group in range(1, 4):
                summed += part_ref[group, yb, side].astype(jnp.float32)
            grad_true = summed[:, :width]
            grad_sample = summed[:, width:]
            state = states_ref[block ^ zh]
            moment_next = momentum_decay * state[1] + (1.0 - momentum_decay) * grad_true
            curvature_next = (
                curvature_decay * state[2] + (1.0 - curvature_decay) * grad_sample * grad_sample
            )
            ratio = jnp.clip(moment_next / (clip_scale * curvature_next), -1.0, 1.0)
            master_next = state[0] * (1.0 - learn_rate * weight_decay) - learn_rate * ratio
            weights = master_next.astype(jnp.bfloat16)
            for copy in range(weights_ref.shape[0]):
                weights_ref[copy, block] = weights

            @pl.when(block == zh)
            def _():
                master_ref[...] = master_next
                moment_ref[...] = moment_next
                curvature_ref[...] = curvature_next


def update(place, part, states):
    rows, width = states.shape[2:]
    whole = pl.BlockSpec(memory_space=pltpu.VMEM)
    mine = jax.ShapeDtypeStruct((rows, width), jnp.float32)
    return pl.pallas_call(
        update_kernel,
        in_specs=[pl.BlockSpec(memory_space=pltpu.SMEM), whole, whole],
        out_specs=[whole] * 4,
        out_shape=[mine, mine, mine, jax.ShapeDtypeStruct((16, 4, rows, width), jnp.bfloat16)],
        compiler_params=pltpu.CompilerParams(vmem_limit_bytes=16 * 1024 * 1024),
        cost_estimate=pl.CostEstimate(flops=2**21, bytes_accessed=2**21, transcendentals=0),
    )(place, part, states)


def shards(
    activations, query_rows, key_rows, true_cotangent, sample_cotangent, master, moment, curvature
):
    zh, core = lax.axis_index("zh"), lax.axis_index("c")
    yl, ya, yb = lax.axis_index("yl"), lax.axis_index("ya"), lax.axis_index("yb")
    rows, width = master.shape
    pair = 2 * width
    across = swap(activations, ("ya", "yb"), 4, 3)
    sibling = swap(activations, "c", 2, 1)
    own = attention_grads(query_rows, key_rows, true_cotangent, sample_cotangent)
    state = jnp.stack((master, moment, curvature))
    own, state = lax.optimization_barrier((own, state))
    other = swap(own, "yb", 2, 1)
    moved = tuple(swap(state, "zh", 4, flip) for flip in (1, 2, 3))
    other, across, moved = lax.optimization_barrier((other, across, moved))
    states = jnp.stack((state,) + moved)

    def whole(half, sibling):
        return jnp.concatenate(
            (jnp.where(core == 0, half, sibling), jnp.where(core == 0, sibling, half)), axis=1
        )

    blocks = whole(activations, sibling), whole(across, swap(across, "c", 2, 1))
    contract = (((0,), (0,)), ((), ()))
    part = [
        lax.dot_general(block, grads, contract, preferred_element_type=jnp.float32)
        for grads in (own, other)
        for block in blocks
    ]
    part = jnp.stack([p.astype(jnp.bfloat16).reshape(16, rows, pair) for p in part], axis=1)
    part, states, place, even = lax.optimization_barrier(
        (part, states, jnp.stack((zh, ya)).astype(jnp.int32), yb == 0)
    )
    part = exchange(part, NEAR)
    part = jnp.sum(part.astype(jnp.float32), axis=0).astype(jnp.bfloat16)
    part_own, part_other = part[:2], part[2:]
    part = jnp.stack(
        (jnp.where(even, part_own, part_other), jnp.where(even, part_other, part_own))
    )
    part = jnp.broadcast_to(part[None], (4, 2, 2, rows, pair)).reshape(8, 2, rows, pair)
    part = exchange(part, ("zh", "yb"))
    *ours, weights = update(place, part.reshape(4, 2, 2, rows, pair), states)
    weights = exchange(weights, NEAR)
    weights_next = weights.transpose(1, 0, 2, 3).reshape(64 * rows, width)
    return (*ours, weights_next)


def solution(mesh):
    fine = Mesh(mesh.devices.reshape(SIZES), AXES)
    dp, mp = AXES[:4], AXES[4:]
    placed = (P(dp, mp),) * 8
    return jax.shard_map(
        shards,
        mesh=fine,
        in_specs=placed,
        out_specs=(P(dp, mp), P(dp, mp), P(dp, mp), P(None, mp)),
        check_vma=False,
    )
```

```python
import math

import jax
import jax.numpy as jnp
from jax import lax
from jax.experimental import pallas as pl
from jax.experimental.pallas import tpu as pltpu
from jax.sharding import Mesh, PartitionSpec as P

HD = 128
TILE = 256

AXES = ("zh", "zl", "yl", "x", "ya", "yb", "c")
SIZES = (4, 2, 2, 4, 2, 2, 2)
NEAR = ("zl", "x", "yl")

momentum_decay = 0.965
curvature_decay = 0.99
clip_scale = 0.04
learn_rate = 0.0006
weight_decay = 0.1


def swap(v, axes, size, flip):
    return lax.ppermute(v, axes, [(i, i ^ flip) for i in range(size)])


def exchange(v, axes):
    return lax.all_to_all(v, axes, 0, 0, tiled=True)


def copies(v, count):
    return jnp.broadcast_to(v[None], (count,) + v.shape)


def attention_kernel(query_ref, key_ref, true_ref, sample_ref, grads_ref):
    tok_count, heads = query_ref.shape[0], query_ref.shape[1] // HD
    to_power = HD ** (-0.5) * math.log2(math.e)
    tiles = tok_count // TILE
    later = lax.broadcasted_iota(jnp.int32, (TILE, TILE), 0) > lax.broadcasted_iota(
        jnp.int32, (TILE, TILE), 1
    )
    totals = [None] * tiles
    for tile in range(tiles):
        start, end = tile * TILE, (tile + 1) * TILE
        attention, cotangents = [], []
        for head in range(heads):
            lanes = slice(head * HD, (head + 1) * HD)
            scores = lax.dot_general(
                key_ref[:end, :],
                query_ref[start:end, lanes],
                (((1,), (1,)), ((), ())),
                preferred_element_type=jnp.float32,
            )
            diagonal = jnp.where(later, -jnp.inf, scores[start:])
            scores = jnp.concatenate((scores[:start], diagonal), axis=0) if start else diagonal
            highest = jnp.max(scores, axis=0, keepdims=True)
            powers = jnp.exp2((scores - highest) * to_power)
            inverse = 1.0 / jnp.sum(powers, axis=0, keepdims=True)
            attention.append((powers * inverse).astype(jnp.bfloat16))
            cotangents.append(
                jnp.concatenate((true_ref[start:end, lanes], sample_ref[start:end, lanes]), axis=1)
            )
        sums = jnp.dot(
            jnp.concatenate(attention, axis=1),
            jnp.concatenate(cotangents, axis=0),
            preferred_element_type=jnp.float32,
        )
        for i in range(tile + 1):
            rows = sums[i * TILE : (i + 1) * TILE]
            totals[i] = rows if totals[i] is None else totals[i] + rows
    for i in range(tiles):
        grads_ref[i * TILE : (i + 1) * TILE, :] = totals[i].astype(grads_ref.dtype)


def attention_grads(query_rows, key_rows, true_cotangent, sample_cotangent):
    whole = pl.BlockSpec(memory_space=pltpu.VMEM)
    return pl.pallas_call(
        attention_kernel,
        in_specs=[whole] * 4,
        out_specs=whole,
        out_shape=jax.ShapeDtypeStruct((key_rows.shape[0], 2 * HD), jnp.bfloat16),
        compiler_params=pltpu.CompilerParams(vmem_limit_bytes=60 * 1024 * 1024),
        cost_estimate=pl.CostEstimate(flops=0, bytes_accessed=0, transcendentals=0),
    )(query_rows, key_rows, true_cotangent, sample_cotangent)


def products_kernel(
    core_ref, own, own_sibling, across, across_sibling, grads, other, part, halves, both, sums, sems
):
    rows, pair = sums.shape[3:]
    loads = [
        pltpu.make_async_copy(grads, both.at[:, :pair], sems.at[4]),
        pltpu.make_async_copy(other, both.at[:, pair:], sems.at[5]),
    ]
    for i, half in enumerate((own, own_sibling, across, across_sibling)):
        loads.append(pltpu.make_async_copy(half, halves.at[i], sems.at[i]))
    for load in loads:
        load.start()
    loads[0].wait()
    loads[1].wait()
    stores = []
    for i in range(4):
        loads[2 + i].wait()
        summed = lax.dot_general(
            halves[i], both[...], (((0,), (0,)), ((), ())), preferred_element_type=jnp.float32
        ).astype(sums.dtype)
        for block in range(8):
            yl, x = block // 4, block % 4
            for head in range(2):
                sums[i, 2 * x + yl, head] = summed[
                    block * rows : (block + 1) * rows, head * pair : (head + 1) * pair
                ]
        side, zl = i // 2, core_ref[0] ^ (i % 2)
        stores.append(
            pltpu.make_async_copy(sums.at[i], part.at[pl.ds(8 * zl, 8), :, side], sems.at[6 + i])
        )
        stores[-1].start()
    for store in stores:
        store.wait()


def products(core, own_block, across_block, own, other):
    anywhere = pl.BlockSpec(memory_space=pl.ANY)
    tok_count, half = own_block[0].shape
    pair = own.shape[1]
    rows = half // 8
    return pl.pallas_call(
        products_kernel,
        in_specs=[pl.BlockSpec(memory_space=pltpu.SMEM)] + [anywhere] * 6,
        out_specs=anywhere,
        out_shape=jax.ShapeDtypeStruct((16, 2, 2, rows, pair), jnp.bfloat16),
        scratch_shapes=[
            pltpu.VMEM((4, tok_count, half), jnp.bfloat16),
            pltpu.VMEM((tok_count, 2 * pair), jnp.bfloat16),
            pltpu.VMEM((4, 8, 2, rows, pair), jnp.bfloat16),
            pltpu.SemaphoreType.DMA((10,)),
        ],
        compiler_params=pltpu.CompilerParams(vmem_limit_bytes=60 * 1024 * 1024),
        cost_estimate=pl.CostEstimate(flops=2**31, bytes_accessed=2**22, transcendentals=0),
    )(core.astype(jnp.int32)[None], *own_block, *across_block, own, other)


def update_kernel(place_ref, part_ref, states_ref, master_ref, moment_ref, curvature_ref, weights_ref):
    zh, ya = place_ref[0], place_ref[1]
    width = master_ref.shape[1]
    for yb in range(2):
        for side in range(2):
            block = (2 * ya + yb) ^ (3 * side)
            summed = part_ref[0, yb, side].astype(jnp.float32)
            for group in range(1, 4):
                summed += part_ref[group, yb, side].astype(jnp.float32)
            grad_true = summed[:, :width]
            grad_sample = summed[:, width:]
            state = states_ref[block ^ zh]
            moment_next = momentum_decay * state[1] + (1.0 - momentum_decay) * grad_true
            curvature_next = (
                curvature_decay * state[2] + (1.0 - curvature_decay) * grad_sample * grad_sample
            )
            ratio = jnp.clip(moment_next / (clip_scale * curvature_next), -1.0, 1.0)
            master_next = state[0] * (1.0 - learn_rate * weight_decay) - learn_rate * ratio
            weights = master_next.astype(jnp.bfloat16)
            for copy in range(weights_ref.shape[0]):
                weights_ref[copy, block] = weights

            @pl.when(block == zh)
            def _():
                master_ref[...] = master_next
                moment_ref[...] = moment_next
                curvature_ref[...] = curvature_next


def update(place, part, states):
    rows, width = states.shape[2:]
    whole = pl.BlockSpec(memory_space=pltpu.VMEM)
    mine = jax.ShapeDtypeStruct((rows, width), jnp.float32)
    return pl.pallas_call(
        update_kernel,
        in_specs=[pl.BlockSpec(memory_space=pltpu.SMEM), whole, whole],
        out_specs=[whole] * 4,
        out_shape=[mine, mine, mine, jax.ShapeDtypeStruct((16, 4, rows, width), jnp.bfloat16)],
        compiler_params=pltpu.CompilerParams(vmem_limit_bytes=16 * 1024 * 1024),
        cost_estimate=pl.CostEstimate(flops=2**21, bytes_accessed=2**21, transcendentals=0),
    )(place, part, states)


def shards(
    activations, query_rows, key_rows, true_cotangent, sample_cotangent, master, moment, curvature
):
    zh, core = lax.axis_index("zh"), lax.axis_index("c")
    yl, ya, yb = lax.axis_index("yl"), lax.axis_index("ya"), lax.axis_index("yb")
    rows, width = master.shape
    pair = 2 * width
    across = swap(activations, ("ya", "yb"), 4, 3)
    sibling = swap(activations, "c", 2, 1)
    own = attention_grads(query_rows, key_rows, true_cotangent, sample_cotangent)
    state = jnp.stack((master, moment, curvature))
    own, state = lax.optimization_barrier((own, state))
    other = swap(own, "yb", 2, 1)
    moved = tuple(swap(state, "zh", 4, flip) for flip in (1, 2, 3))
    other, across, moved = lax.optimization_barrier((other, across, moved))
    states = jnp.stack((state,) + moved)

    part = products(core, (activations, sibling), (across, swap(across, "c", 2, 1)), own, other)
    part = part.reshape(16, 4, rows, pair)
    part, states, place, even = lax.optimization_barrier(
        (part, states, jnp.stack((zh, ya)).astype(jnp.int32), yb == 0)
    )
    part = exchange(part, NEAR)
    part = jnp.sum(part.astype(jnp.float32), axis=0).astype(jnp.bfloat16)
    part_own, part_other = part[:2], part[2:]
    part = jnp.stack(
        (jnp.where(even, part_own, part_other), jnp.where(even, part_other, part_own))
    )
    part = jnp.broadcast_to(part[None], (4, 2, 2, rows, pair)).reshape(8, 2, rows, pair)
    part = exchange(part, ("zh", "yb"))
    *ours, weights = update(place, part.reshape(4, 2, 2, rows, pair), states)
    weights = exchange(weights, NEAR)
    weights_next = weights.reshape(2, 4, 2, 4, rows, width).transpose(3, 0, 2, 1, 4, 5)
    weights_next = weights_next.reshape(64 * rows, width)
    return (*ours, weights_next)


def solution(mesh):
    fine = Mesh(mesh.devices.reshape(SIZES), AXES)
    dp, mp = AXES[:4], AXES[4:]
    placed = (P(dp, mp),) * 8
    return jax.shard_map(
        shards,
        mesh=fine,
        in_specs=placed,
        out_specs=(P(dp, mp), P(dp, mp), P(dp, mp), P(None, mp)),
        check_vma=False,
    )
```

```python
import math

import jax
import jax.numpy as jnp
from jax import lax
from jax.experimental import pallas as pl
from jax.experimental.pallas import tpu as pltpu
from jax.sharding import Mesh, PartitionSpec as P

HD = 128
TILE = 256

AXES = ("zh", "zl", "yl", "x", "ya", "yb", "c")
SIZES = (4, 2, 2, 4, 2, 2, 2)
NEAR = ("zl", "yl", "x")

momentum_decay = 0.965
curvature_decay = 0.99
clip_scale = 0.04
learn_rate = 0.0006
weight_decay = 0.1


def swap(v, axes, size, flip):
    return lax.ppermute(v, axes, [(i, i ^ flip) for i in range(size)])


def exchange(v, axes):
    return lax.all_to_all(v, axes, 0, 0, tiled=True)


def copies(v, count):
    return jnp.broadcast_to(v[None], (count,) + v.shape)


def attention_kernel(query_ref, key_ref, true_ref, sample_ref, grads_ref):
    tok_count, heads = query_ref.shape[0], query_ref.shape[1] // HD
    to_power = HD ** (-0.5) * math.log2(math.e)
    tiles = tok_count // TILE
    later = lax.broadcasted_iota(jnp.int32, (TILE, TILE), 0) > lax.broadcasted_iota(
        jnp.int32, (TILE, TILE), 1
    )
    totals = [None] * tiles
    for tile in range(tiles):
        start, end = tile * TILE, (tile + 1) * TILE
        attention, cotangents = [], []
        for head in range(heads):
            lanes = slice(head * HD, (head + 1) * HD)
            scores = lax.dot_general(
                key_ref[:end, :],
                query_ref[start:end, lanes],
                (((1,), (1,)), ((), ())),
                preferred_element_type=jnp.float32,
            )
            diagonal = jnp.where(later, -jnp.inf, scores[start:])
            scores = jnp.concatenate((scores[:start], diagonal), axis=0) if start else diagonal
            highest = jnp.max(scores, axis=0, keepdims=True)
            powers = jnp.exp2((scores - highest) * to_power)
            inverse = 1.0 / jnp.sum(powers, axis=0, keepdims=True)
            attention.append((powers * inverse).astype(jnp.bfloat16))
            cotangents.append(
                jnp.concatenate((true_ref[start:end, lanes], sample_ref[start:end, lanes]), axis=1)
            )
        sums = jnp.dot(
            jnp.concatenate(attention, axis=1),
            jnp.concatenate(cotangents, axis=0),
            preferred_element_type=jnp.float32,
        )
        for i in range(tile + 1):
            rows = sums[i * TILE : (i + 1) * TILE]
            totals[i] = rows if totals[i] is None else totals[i] + rows
    for i in range(tiles):
        grads_ref[i * TILE : (i + 1) * TILE, :] = totals[i].astype(grads_ref.dtype)


def attention_grads(query_rows, key_rows, true_cotangent, sample_cotangent):
    whole = pl.BlockSpec(memory_space=pltpu.VMEM)
    return pl.pallas_call(
        attention_kernel,
        in_specs=[whole] * 4,
        out_specs=whole,
        out_shape=jax.ShapeDtypeStruct((key_rows.shape[0], 2 * HD), jnp.bfloat16),
        compiler_params=pltpu.CompilerParams(vmem_limit_bytes=60 * 1024 * 1024),
        cost_estimate=pl.CostEstimate(flops=0, bytes_accessed=0, transcendentals=0),
    )(query_rows, key_rows, true_cotangent, sample_cotangent)


def update_kernel(place_ref, part_ref, states_ref, master_ref, moment_ref, curvature_ref, weights_ref):
    zh, ya = place_ref[0], place_ref[1]
    width = master_ref.shape[1]
    for yb in range(2):
        for side in range(2):
            block = (2 * ya + yb) ^ (3 * side)
            summed = part_ref[0, yb, side].astype(jnp.float32)
            for group in range(1, 4):
                summed += part_ref[group, yb, side].astype(jnp.float32)
            grad_true = summed[:, :width]
            grad_sample = summed[:, width:]
            state = states_ref[block ^ zh]
            moment_next = momentum_decay * state[1] + (1.0 - momentum_decay) * grad_true
            curvature_next = (
                curvature_decay * state[2] + (1.0 - curvature_decay) * grad_sample * grad_sample
            )
            ratio = jnp.clip(moment_next / (clip_scale * curvature_next), -1.0, 1.0)
            master_next = state[0] * (1.0 - learn_rate * weight_decay) - learn_rate * ratio
            weights = master_next.astype(jnp.bfloat16)
            for copy in range(weights_ref.shape[0]):
                weights_ref[copy, block] = weights

            @pl.when(block == zh)
            def _():
                master_ref[...] = master_next
                moment_ref[...] = moment_next
                curvature_ref[...] = curvature_next


def update(place, part, states):
    rows, width = states.shape[2:]
    whole = pl.BlockSpec(memory_space=pltpu.VMEM)
    mine = jax.ShapeDtypeStruct((rows, width), jnp.float32)
    return pl.pallas_call(
        update_kernel,
        in_specs=[pl.BlockSpec(memory_space=pltpu.SMEM), whole, whole],
        out_specs=[whole] * 4,
        out_shape=[mine, mine, mine, jax.ShapeDtypeStruct((16, 4, rows, width), jnp.bfloat16)],
        compiler_params=pltpu.CompilerParams(vmem_limit_bytes=16 * 1024 * 1024),
        cost_estimate=pl.CostEstimate(flops=2**21, bytes_accessed=2**21, transcendentals=0),
    )(place, part, states)


def shards(
    activations, query_rows, key_rows, true_cotangent, sample_cotangent, master, moment, curvature
):
    zh, core = lax.axis_index("zh"), lax.axis_index("c")
    yl, ya, yb = lax.axis_index("yl"), lax.axis_index("ya"), lax.axis_index("yb")
    rows, width = master.shape
    pair = 2 * width
    across = swap(activations, ("ya", "yb"), 4, 3)
    own = attention_grads(query_rows, key_rows, true_cotangent, sample_cotangent)
    state = jnp.stack((master, moment, curvature))
    own, state, halves = lax.optimization_barrier((own, state, activations))
    sibling = swap(halves, "c", 2, 1)
    other = swap(own, "yb", 2, 1)
    moved = tuple(swap(state, "zh", 4, flip) for flip in (1, 2, 3))
    other, across, moved = lax.optimization_barrier((other, across, moved))
    states = jnp.stack((state,) + moved)

    def whole(half, sibling):
        return jnp.concatenate(
            (jnp.where(core == 0, half, sibling), jnp.where(core == 0, sibling, half)), axis=1
        )

    blocks = whole(activations, sibling), whole(across, swap(across, "c", 2, 1))
    contract = (((0,), (0,)), ((), ()))
    part = [
        lax.dot_general(block, grads, contract, preferred_element_type=jnp.float32)
        for grads in (own, other)
        for block in blocks
    ]
    part = jnp.stack([p.astype(jnp.bfloat16).reshape(16, rows, pair) for p in part], axis=1)
    part, states, place, even = lax.optimization_barrier(
        (part, states, jnp.stack((zh, ya)).astype(jnp.int32), yb == 0)
    )
    part = exchange(part, NEAR)
    part = jnp.sum(part.astype(jnp.float32), axis=0).astype(jnp.bfloat16)
    part_own, part_other = part[:2], part[2:]
    part = jnp.stack(
        (jnp.where(even, part_own, part_other), jnp.where(even, part_other, part_own))
    )
    part = jnp.broadcast_to(part[None], (4, 2, 2, rows, pair)).reshape(8, 2, rows, pair)
    part = exchange(part, ("zh", "yb"))
    *ours, weights = update(place, part.reshape(4, 2, 2, rows, pair), states)
    weights = exchange(weights, ("zl", "x", "yl"))
    weights_next = weights.reshape(2, 4, 2, 4, rows, width).transpose(3, 0, 2, 1, 4, 5)
    weights_next = weights_next.reshape(64 * rows, width)
    return (*ours, weights_next)


def solution(mesh):
    fine = Mesh(mesh.devices.reshape(SIZES), AXES)
    dp, mp = AXES[:4], AXES[4:]
    placed = (P(dp, mp),) * 8
    return jax.shard_map(
        shards,
        mesh=fine,
        in_specs=placed,
        out_specs=(P(dp, mp), P(dp, mp), P(dp, mp), P(None, mp)),
        check_vma=False,
    )
```
